32 devices in a mesh: row: 4 (over y, x), col: 8 (over z, core).
Axes of the slice: x: 2, y: 2, z: 4, core: 2. Of those that a mesh axis runs over, the one named last changes fastest.
Arguments:
- out_grad: bfloat16 [512, 8192], P('col', 'row'), may hold values from -6 to 6
- hidden: bfloat16 [512, 28672], P('row', 'col'), may hold values from -0.12988281 to 0.12988281
- weight: bfloat16 [28672, 8192], P('col', 'row'), may hold values from -0.03125 to 0.03125
Outputs:
- token_grad: bfloat16 [512, 28672], P('row', 'col')
- weight_grad: bfloat16 [28672, 8192], P('col', 'row')
The draws below stay inside these ranges and needn't reach their ends.
All inputs are finite; a program needn't handle non-finite values.
Results may differ from the reference program's by a relative error of at most 0.001.
Values may be sent and summed in bfloat16 or wider, within the bound.
No kernel may reach another device: no remote copies, remote signals or barrier semaphores. Data moves between devices by JAX's collectives and lax.ppermute only.
A program may use at most 192 MiB of HBM per device.

```python
import jax
import jax.numpy as jnp

D = 8192
FF = 28672
TOKENS = 512


def spiked(array, stream_key, source, target, parts, factor):
    def block_of(axis_at):
        return (jnp.arange(array.shape[axis_at]) // (array.shape[axis_at] // parts)).reshape((-1,) + (1,) * (array.ndim - 1 - axis_at))

    near = jax.random.permutation(stream_key, parts)[block_of(target)]
    second = (block_of(target) + parts // 2) % parts
    return jnp.where((block_of(source) == near) | (block_of(source) == second), factor * array, array)


def level_of(own_key, shape, split, smallest, top_value):
    gain, own = 1.0, jax.random.fold_in(own_key, 6)
    for position, blocks in split:
        steps = jnp.exp(jax.random.uniform(jax.random.fold_in(own, position), (blocks,), jnp.float32, smallest / len(split), top_value / len(split)))
        gain = gain * jnp.repeat(steps, shape[position] // blocks).reshape([-1 if axis == position else 1 for axis in range(len(shape))])
    return gain


def bell_draw(key, shape, spread, bound, cuts=(), kind=jnp.bfloat16):
    drawn = spread * jax.random.normal(key, shape, jnp.float32)
    if cuts:
        drawn = drawn * level_of(key, shape, cuts, -0.22, 0.18)
    return jnp.clip(drawn, -bound, bound).astype(kind)


def gaussian_with(stream_key, extent, width, reach, split, heavy, dtype=jnp.bfloat16):
    drawn = width * jax.random.normal(stream_key, extent, jnp.float32)
    if split:
        drawn = drawn * level_of(stream_key, extent, split, -0.22, 0.18)
    return jnp.clip(spiked(drawn, jax.random.fold_in(stream_key, 3), *heavy), -reach, reach).astype(dtype)


def setup_inputs(seed: int = 0) -> dict:
    streams_of = jax.random.split(jax.random.key(seed), 4)
    return {
        "out_grad": gaussian_with(streams_of[0], (TOKENS, D), 1.0, 6.0, ((0, 8), (1, 4)), (1, 0, 8, 2.0)),
        "hidden": bell_draw(streams_of[1], (TOKENS, FF), 0.022, 0.12988281, ((0, 4), (1, 8))),
        "weight": bell_draw(streams_of[2], (FF, D), FF ** -0.5, 0.03125, ((0, 8), (1, 4))),
    }


def reference(out_grad, hidden, weight):
    token_grad = jnp.dot(out_grad, weight.T, preferred_element_type=jnp.float32).astype(jnp.bfloat16)
    weight_grad = jnp.dot(hidden.T, out_grad, preferred_element_type=jnp.float32).astype(jnp.bfloat16)
    return token_grad, weight_grad
```

```python
import functools

import jax
import jax.numpy as jnp
from jax import lax
from jax.experimental import pallas as pl
from jax.experimental.pallas import tpu as pltpu
from jax.sharding import PartitionSpec as P

CORES = 2
SPAN = 120.0
SCALE_ROWS = 16
VMEM = 56 * 1024 * 1024


def grid_of(n):
    ny = int(n**0.5)
    while n % ny:
        ny -= 1
    return ny, n // ny


def encode(block):
    top = jnp.max(jnp.abs(block), axis=0, keepdims=True)
    scale = jnp.maximum(top * 1.0078125, 1e-36).astype(jnp.bfloat16)
    level = jnp.abs(block) * (2 * SPAN / scale.astype(jnp.float32)) - SPAN
    size = jnp.exp2(level)
    return jnp.where(block < 0, -size, size).astype(jnp.bfloat16), scale


def decode(code, scale):
    value = code.astype(jnp.float32)
    size = (jnp.log2(jnp.abs(value)) + SPAN) * (scale.astype(jnp.float32)[:1] * (0.5 / SPAN))
    return jnp.where(value < 0, -size, size)


def store_message(ref, block):
    rows = block.shape[0]
    code, scale = encode(block)
    ref[:rows, :] = code
    ref[rows:, :] = jnp.broadcast_to(scale, (SCALE_ROWS, block.shape[1]))


class Plan:
    def __init__(self, mesh):
        self.n, self.m = mesh.shape["row"], mesh.shape["col"]
        self.ny, self.nx = grid_of(self.n)
        self.nz = self.m // CORES

    def place(self):
        row, col = lax.axis_index("row"), lax.axis_index("col")
        return row // self.nx, row % self.nx, col // CORES, col % CORES

    def send_row(self, array, dy, dx):
        ny, nx = self.ny, self.nx
        pairs = [(y * nx + x, (y + dy) % ny * nx + (x + dx) % nx) for y in range(ny) for x in range(nx)]
        return lax.ppermute(array, "row", pairs)

    def peer_z(self, z, d):
        return z ^ d if self.nz & (self.nz - 1) == 0 else (z + d) % self.nz

    def from_z(self, z, d):
        return z ^ d if self.nz & (self.nz - 1) == 0 else (z + self.nz - d) % self.nz

    def send_z(self, array, d):
        pairs = [(z * CORES + c, self.peer_z(z, d) * CORES + c) for z in range(self.nz) for c in range(CORES)]
        return lax.ppermute(array, "col", pairs)

    def swap(self, array, d):
        pairs = [(z * CORES + c, z * CORES + (c + d) % CORES) for z in range(self.nz) for c in range(CORES)]
        return lax.ppermute(array, "col", pairs)

    def load_tokens(self, pieces, held, sems, x_major):
        y, x, z, core = self.place()
        rows = pieces[0].shape[0]
        per = self.m // self.n
        copies = []
        for at in range(len(pieces)):
            d, c = at // CORES, at % CORES
            origin = self.from_z(z, d) * CORES + lax.rem(core + CORES - c, CORES)
            owner = origin // per
            dy = lax.rem(owner // self.nx + self.ny - y, self.ny)
            dx = lax.rem(owner % self.nx + self.nx - x, self.nx)
            slot = dx * self.ny + dy if x_major else dy * self.nx + dx
            start = pl.multiple_of((slot * per + origin % per) * rows, rows)
            copies.append(pltpu.make_async_copy(pieces[at], held.at[pl.ds(start, rows), :], sems.at[at]))
        for copy in copies:
            copy.start()
        for copy in copies:
            copy.wait()

    def token_part(self, pieces, weight, first, width, tile, x_first):
        count, (rows, depth) = len(pieces), pieces[0].shape
        tokens = count * rows
        own = tokens // self.n
        peers, blocks = (self.nx, self.ny) if x_first else (self.ny, self.nx)
        group = blocks * own

        def kernel(*refs):
            parts, weight_ref = refs[:count], refs[count]
            messages, keep = refs[count + 1 : count + peers], refs[count + peers]
            held, sems = refs[-2:]

            @pl.when(pl.program_id(0) == 0)
            def _():
                self.load_tokens(parts, held, sems, x_first)

            total = lax.dot_general(
                held[...], weight_ref[...], (((1,), (1,)), ((), ())), preferred_element_type=jnp.float32
            )
            keep[...] = total[:group]
            for peer in range(1, peers):
                store_message(messages[peer - 1], total[peer * group : (peer + 1) * group])

        message = jax.ShapeDtypeStruct((group + SCALE_ROWS, width), jnp.bfloat16)
        out = pl.pallas_call(
            kernel,
            grid=(width // tile,),
            in_specs=[pl.BlockSpec(memory_space=pl.ANY)] * count
            + [pl.BlockSpec((tile, depth), lambda i: (first // tile + i, 0))],
            out_specs=[pl.BlockSpec((group + SCALE_ROWS, tile), lambda i: (0, i))] * (peers - 1)
            + [pl.BlockSpec((group, tile), lambda i: (0, i))],
            out_shape=[message] * (peers - 1) + [jax.ShapeDtypeStruct((group, width), jnp.float32)],
            scratch_shapes=[pltpu.VMEM((tokens, depth), jnp.bfloat16), pltpu.SemaphoreType.DMA((count,))],
            compiler_params=pltpu.CompilerParams(vmem_limit_bytes=VMEM),
            cost_estimate=pl.CostEstimate(
                flops=2 * tokens * depth * width,
                bytes_accessed=2 * (tokens + width) * depth + 4 * tokens * width,
                transcendentals=tokens * width,
            ),
            name="token_part",
        )(*pieces, weight)
        return out[:-1], out[-1]

    def combine(self, got, keep, blocks):
        count, width = len(got), keep.shape[1]
        group = keep.shape[0]
        own = group // blocks

        def kernel(*refs):
            messages, keep_ref, outs = refs[:count], refs[count], refs[count + 1 :]
            for block in range(1, blocks):
                rows = slice(block * own, (block + 1) * own)
                total = keep_ref[rows, :]
                for message in messages:
                    total = total + decode(message[rows, :], message[group:, :])
                store_message(outs[block - 1], total)

        tile = width
        return pl.pallas_call(
            kernel,
            grid=(width // tile,),
            in_specs=[pl.BlockSpec((group + SCALE_ROWS, tile), lambda i: (0, i))] * count
            + [pl.BlockSpec((group, tile), lambda i: (0, i))],
            out_specs=[pl.BlockSpec((own + SCALE_ROWS, tile), lambda i: (0, i))] * (blocks - 1),
            out_shape=[jax.ShapeDtypeStruct((own + SCALE_ROWS, width), jnp.bfloat16)] * (blocks - 1),
            compiler_params=pltpu.CompilerParams(vmem_limit_bytes=VMEM),
            cost_estimate=pl.CostEstimate(
                flops=20 * group * width, bytes_accessed=8 * group * width, transcendentals=2 * group * width
            ),
            name="combine",
        )(*got, keep)

    def finish(self, chunks, own):
        total_width = sum(chunk[1] for chunk in chunks)
        operands, in_specs = [], []
        for first, width, keep, got, late in chunks:
            group = keep.shape[0]
            operands.append(keep)
            in_specs.append(pl.BlockSpec((own, width), lambda i: (0, 0)))
            for array in got:
                operands += [array, array]
                in_specs.append(pl.BlockSpec((own, width), lambda i: (0, 0)))
                in_specs.append(pl.BlockSpec((SCALE_ROWS, width), lambda i, at=group // SCALE_ROWS: (at, 0)))
            for array in late:
                operands.append(array)
                in_specs.append(pl.BlockSpec((own + SCALE_ROWS, width), lambda i: (0, 0)))

        def kernel(*refs):
            out, at = refs[-1], 0
            for first, width, keep, got, late in chunks:
                total = refs[at][...]
                at += 1
                for _ in got:
                    total = total + decode(refs[at][...], refs[at + 1][...])
                    at += 2
                for _ in late:
                    total = total + decode(refs[at][:own, :], refs[at][own:, :])
                    at += 1
                out[:, first : first + width] = total.astype(jnp.bfloat16)

        return pl.pallas_call(
            kernel,
            grid=(1,),
            in_specs=in_specs,
            out_specs=pl.BlockSpec((own, total_width), lambda i: (0, 0)),
            out_shape=jax.ShapeDtypeStruct((own, total_width), jnp.bfloat16),
            compiler_params=pltpu.CompilerParams(vmem_limit_bytes=VMEM),
            cost_estimate=pl.CostEstimate(
                flops=30 * own * total_width, bytes_accessed=12 * own * total_width, transcendentals=2 * own * total_width
            ),
            name="finish",
        )(*operands)

    def weight_part(self, pieces, blocks, tile):
        count, (rows, width) = len(pieces), pieces[0].shape
        tokens = count * rows
        units = blocks[0].shape[1]
        many = len(blocks)

        def kernel(*refs):
            parts, hidden = refs[:count], refs[count : count + many]
            out, held, sems = refs[count + many :]

            @pl.when(pl.program_id(0) == 0)
            def _():
                self.load_tokens(parts, held, sems, False)

            full = jnp.concatenate([ref[...] for ref in hidden], axis=0)
            out[...] = lax.dot_general(
                full, held[...], (((0,), (0,)), ((), ())), preferred_element_type=jnp.float32
            ).astype(jnp.bfloat16)

        return pl.pallas_call(
            kernel,
            grid=(units // tile,),
            in_specs=[pl.BlockSpec(memory_space=pl.ANY)] * count
            + [pl.BlockSpec((block.shape[0], tile), lambda i: (0, i)) for block in blocks],
            out_specs=pl.BlockSpec((tile, width), lambda i: (i, 0)),
            out_shape=jax.ShapeDtypeStruct((units, width), jnp.bfloat16),
            scratch_shapes=[pltpu.VMEM((tokens, width), jnp.bfloat16), pltpu.SemaphoreType.DMA((count,))],
            compiler_params=pltpu.CompilerParams(vmem_limit_bytes=VMEM),
            cost_estimate=pl.CostEstimate(
                flops=2 * tokens * units * width,
                bytes_accessed=2 * (tokens * (units + width) + units * width),
                transcendentals=0,
            ),
            name="weight_part",
        )(*pieces, *blocks)


def split(total, tile):
    tiles = total // tile
    parts = min(4, tiles)
    sizes = [tiles // parts + (at < tiles % parts) for at in range(parts)]
    chunks, first = [], 0
    for at, size in enumerate(sizes):
        chunks.append((first * tile, size * tile, at % 2 == 0))
        first += size
    return chunks


def on_device(plan, out_grad, hidden, weight):
    ny, nx = plan.ny, plan.nx
    pieces = []
    for d in range(plan.nz):
        piece = plan.send_z(out_grad, d) if d else out_grad
        pieces += [piece] + [plan.swap(piece, c) for c in range(1, CORES)]

    own = hidden.shape[0]
    half = own // 2
    at_x = [hidden] + [plan.send_row(hidden, 0, dx) for dx in range(1, nx)]
    at_y = [hidden] + [plan.send_row(hidden, dy, 0) for dy in range(1, ny)]

    def block_of(dy, dx):
        if dy == 0:
            return [at_x[dx]]
        if dx == 0:
            return [at_y[dy]]
        return [plan.send_row(at_x[dx][:half], dy, 0), plan.send_row(at_y[dy][half:], 0, dx)]

    blocks = []
    for sy in range(ny):
        for sx in range(nx):
            blocks += block_of((ny - sy) % ny, (nx - sx) % nx)

    units = hidden.shape[1]
    tile = 256 if units % 256 == 0 else 128
    parts = []
    for first, width, x_first in split(units, tile):
        messages, keep = plan.token_part(pieces, weight, first, width, tile, x_first)
        got = [plan.send_row(msg, 0, d + 1) if x_first else plan.send_row(msg, d + 1, 0) for d, msg in enumerate(messages)]
        parts.append((first, width, x_first, keep, got))

    weight_grad = plan.weight_part(pieces, blocks, tile)

    chunks = []
    for first, width, x_first, keep, got in parts:
        onward = plan.combine(got, keep, ny if x_first else nx)
        late = [plan.send_row(msg, d + 1, 0) if x_first else plan.send_row(msg, 0, d + 1) for d, msg in enumerate(onward)]
        chunks.append((first, width, keep, got, late))
    return plan.finish(chunks, own), weight_grad


def solution(mesh):
    return jax.shard_map(
        functools.partial(on_device, Plan(mesh)),
        mesh=mesh,
        in_specs=(P("col", "row"), P("row", "col"), P("col", "row")),
        out_specs=(P("row", "col"), P("col", "row")),
        check_vma=False,
    )
```

```python
import functools

import jax
import jax.numpy as jnp
from jax import lax
from jax.experimental import pallas as pl
from jax.experimental.pallas import tpu as pltpu
from jax.sharding import PartitionSpec as P

CORES = 2
SPAN = 120.0
SCALE_ROWS = 16
COST = 1024
SCOPED = 20 * 1024 * 1024
ANY, HBM, VMEM = pl.ANY, pltpu.HBM, pltpu.VMEM
MARK = ((8, 128), jnp.float32, VMEM)


def call(kernel, name, operands, results, scratch=(), aliases={}):
    return pl.pallas_call(
        kernel,
        in_specs=[pl.BlockSpec(memory_space=memory) for _, memory in operands],
        out_specs=[pl.BlockSpec(memory_space=memory) for _, _, memory in results],
        out_shape=[
            jax.ShapeDtypeStruct(shape, dtype) if memory is ANY else memory(shape, dtype)
            for shape, dtype, memory in results
        ],
        scratch_shapes=list(scratch),
        input_output_aliases=aliases,
        compiler_params=pltpu.CompilerParams(vmem_limit_bytes=SCOPED),
        cost_estimate=pl.CostEstimate(flops=COST, bytes_accessed=COST, transcendentals=0),
        name=name,
    )(*[pltpu.with_memory_space_constraint(array, memory) for array, memory in operands])


def grid_of(n):
    ny = int(n**0.5)
    while n % ny:
        ny -= 1
    return ny, n // ny


def encode(blocks):
    top = functools.reduce(jnp.maximum, [jnp.max(jnp.abs(block), axis=0, keepdims=True) for block in blocks])
    scale = jnp.maximum(top * 1.0078125, 1e-36).astype(jnp.bfloat16)
    step = 2 * SPAN / scale.astype(jnp.float32)
    codes = []
    for block in blocks:
        size = jnp.exp2(jnp.abs(block) * step - SPAN)
        codes.append(jnp.where(block < 0, -size, size).astype(jnp.bfloat16))
    return codes, scale


def decode(code, scale):
    value = code.astype(jnp.float32)
    size = (jnp.log2(jnp.abs(value)) + SPAN) * (scale.astype(jnp.float32)[:1] * (0.5 / SPAN))
    return jnp.where(value < 0, -size, size)


def store_message(ref, blocks, columns):
    codes, scale = encode(blocks)
    at = 0
    for code in codes:
        ref[at : at + code.shape[0], columns] = code
        at += code.shape[0]
    ref[at:, columns] = jnp.broadcast_to(scale, (SCALE_ROWS, scale.shape[1]))


class Plan:
    def __init__(self, mesh):
        self.n, self.m = mesh.shape["row"], mesh.shape["col"]
        self.ny, self.nx = grid_of(self.n)
        self.nz = self.m // CORES

    def place(self):
        row, col = lax.axis_index("row"), lax.axis_index("col")
        return row // self.nx, row % self.nx, col // CORES, col % CORES

    def send_row(self, array, dy, dx):
        ny, nx = self.ny, self.nx
        pairs = [(y * nx + x, (y + dy) % ny * nx + (x + dx) % nx) for y in range(ny) for x in range(nx)]
        return lax.ppermute(array, "row", pairs)

    def peer_z(self, z, d):
        return z ^ d if self.nz & (self.nz - 1) == 0 else (z + d) % self.nz

    def from_z(self, z, d):
        return z ^ d if self.nz & (self.nz - 1) == 0 else (z + self.nz - d) % self.nz

    def send_z(self, array, d):
        pairs = [(z * CORES + c, self.peer_z(z, d) * CORES + c) for z in range(self.nz) for c in range(CORES)]
        return lax.ppermute(array, "col", pairs)

    def swap(self, array, d):
        pairs = [(z * CORES + c, z * CORES + (c + d) % CORES) for z in range(self.nz) for c in range(CORES)]
        return lax.ppermute(array, "col", pairs)

    def token_copies(self, pieces, held, sems):
        y, x, z, core = self.place()
        rows = pieces[0].shape[0]
        per = self.m // self.n
        copies = []
        for at in range(len(pieces)):
            d, c = at // CORES, at % CORES
            origin = self.from_z(z, d) * CORES + lax.rem(core + CORES - c, CORES)
            owner = origin // per
            dy = lax.rem(owner // self.nx + self.ny - y, self.ny)
            dx = lax.rem(owner % self.nx + self.nx - x, self.nx)
            start = pl.multiple_of(((dy * self.nx + dx) * per + origin % per) * rows, rows)
            copies.append(pltpu.make_async_copy(pieces[at], held.at[pl.ds(start, rows), :], sems.at[at]))
        return copies

    def stage(self, weight, relay):
        def kernel(weight_ref, *refs):
            out, _, sem = refs[-3:]
            copy = pltpu.make_async_copy(weight_ref, out, sem)
            copy.start()
            copy.wait()

        return call(
            kernel,
            "stage",
            [(weight, HBM), (relay, ANY)],
            [(weight.shape, weight.dtype, VMEM), (relay.shape, relay.dtype, ANY)],
            [pltpu.SemaphoreType.DMA],
            aliases={1: 1},
        )

    def relay(self, array, after):
        operands = [(array, ANY)] + [(other, VMEM) for other in after]
        return call(lambda *refs: None, "relay", operands, [(array.shape, array.dtype, ANY)], aliases={0: 0})[0]

    def gather_tokens(self, pieces, after):
        count, (rows, depth) = len(pieces), pieces[0].shape

        def kernel(*refs):
            out, sems = refs[-2:]
            copies = self.token_copies(refs[:count], out, sems)
            for copy in copies:
                copy.start()
            for copy in copies:
                copy.wait()

        return call(
            kernel,
            "gather_tokens",
            [(piece, ANY) for piece in pieces] + [(array, ANY) for array in after],
            [((count * rows, depth), jnp.bfloat16, VMEM)],
            [pltpu.SemaphoreType.DMA((count,))],
        )[0]

    def gather_hidden(self, blocks, after):
        count, units = len(blocks), blocks[0].shape[1]
        tokens = sum(block.shape[0] for block in blocks)

        def kernel(*refs):
            out, sems = refs[-2:]
            copies, at = [], 0
            for index, ref in enumerate(refs[:count]):
                rows = ref.shape[0]
                copies.append(pltpu.make_async_copy(ref, out.at[pl.ds(at, rows), :], sems.at[index]))
                at += rows
            for copy in copies:
                copy.start()
            for copy in copies:
                copy.wait()

        return call(
            kernel,
            "gather_hidden",
            [(block, ANY) for block in blocks] + [(array, VMEM) for array in after],
            [((tokens, units), jnp.bfloat16, VMEM)],
            [pltpu.SemaphoreType.DMA((count,))],
        )[0]

    def token_part(self, held, weight, first, width, tile, x_first, after):
        tokens, depth = held.shape
        own = tokens // self.n
        peers, blocks = (self.nx, self.ny) if x_first else (self.ny, self.nx)
        group = blocks * own

        def kernel(held_ref, weight_ref, *refs):
            outs = refs[len(after) :]
            messages, keep = outs[:-1], outs[-1]
            for at in range(0, width, tile):
                size = min(tile, width - at)
                columns = slice(at, at + size)
                total = lax.dot_general(
                    held_ref[...],
                    weight_ref[first + at : first + at + size, :],
                    (((1,), (1,)), ((), ())),
                    preferred_element_type=jnp.float32,
                )

                def block(peer, at):
                    slot = at * self.nx + peer if x_first else peer * self.nx + at
                    return total[slot * own : (slot + 1) * own]

                for peer in range(1, peers):
                    store_message(messages[peer - 1], [block(peer, at) for at in range(blocks)], columns)
                for at in range(blocks):
                    keep[at * own : (at + 1) * own, columns] = block(0, at)

        *messages, keep = call(
            kernel,
            "token_part",
            [(held, VMEM), (weight, VMEM)] + [(array, VMEM) for array in after],
            [((group + SCALE_ROWS, width), jnp.bfloat16, VMEM)] * (peers - 1) + [((group, width), jnp.float32, VMEM)],
        )
        return messages, keep

    def combine(self, got, keep, blocks, after):
        count, (group, width) = len(got), keep.shape
        own = group // blocks

        def kernel(*refs):
            messages, keep_ref, outs = refs[:count], refs[count], refs[count + 1 + len(after) :]
            for block in range(1, blocks):
                rows = slice(block * own, (block + 1) * own)
                total = keep_ref[rows, :]
                for message in messages:
                    total = total + decode(message[rows, :], message[group:, :])
                store_message(outs[block - 1], [total], slice(None))

        return call(
            kernel,
            "combine",
            [(array, VMEM) for array in (*got, keep, *after)],
            [((own + SCALE_ROWS, width), jnp.bfloat16, VMEM)] * (blocks - 1),
        )

    def finish(self, first, keep, got, late, own, units, so_far, after):
        group, width = keep.shape
        operands = [(array, VMEM) for array in (keep, *got, *late, *after)]
        extra = [(so_far, HBM)] if so_far is not None else []

        def kernel(*refs):
            total = refs[0][:own, :]
            for message in refs[1 : 1 + len(got)]:
                total = total + decode(message[:own, :], message[group:, :])
            for message in refs[1 + len(got) : 1 + len(got) + len(late)]:
                total = total + decode(message[:own, :], message[own:, :])
            out, _, buf, sem = refs[-4:]
            buf[...] = total.astype(jnp.bfloat16)
            copy = pltpu.make_async_copy(buf, out.at[:, pl.ds(first, width)], sem)
            copy.start()
            copy.wait()

        return call(
            kernel,
            "finish",
            operands + extra,
            [((own, units), jnp.bfloat16, HBM), MARK],
            [pltpu.VMEM((own, width), jnp.bfloat16), pltpu.SemaphoreType.DMA],
            aliases={len(operands): 0} if extra else {},
        )

    def weight_part(self, held, hidden, first, width, tile, so_far, after):
        (tokens, depth), units = held.shape, hidden.shape[1]
        steps = width // tile
        extra = [(so_far, HBM)] if so_far is not None else []
        operands = [(array, VMEM) for array in (held, hidden, *after)]

        def kernel(held_ref, hidden_ref, *refs):
            out, _, buf, sems = refs[-4:]
            pending = []
            for s in range(steps):
                if s >= 2:
                    pending[s - 2].wait()
                start = first + s * tile
                buf[s % 2] = lax.dot_general(
                    hidden_ref[:, start : start + tile],
                    held_ref[...],
                    (((0,), (0,)), ((), ())),
                    preferred_element_type=jnp.float32,
                ).astype(jnp.bfloat16)
                pending.append(pltpu.make_async_copy(buf.at[s % 2], out.at[pl.ds(start, tile), :], sems.at[s % 2]))
                pending[-1].start()
            for copy in pending[-2:]:
                copy.wait()

        return call(
            kernel,
            "weight_part",
            operands + extra,
            [((units, depth), jnp.bfloat16, HBM), MARK],
            [pltpu.VMEM((2, tile, depth), jnp.bfloat16), pltpu.SemaphoreType.DMA((2,))],
            aliases={len(operands): 0} if extra else {},
        )


def split(total, tile, parts):
    tiles = total // tile
    parts = min(parts, tiles)
    sizes = [tiles // parts + (at < tiles % parts) for at in range(parts)]
    return [(sum(sizes[:at]) * tile, size * tile) for at, size in enumerate(sizes)]


def on_device(plan, out_grad, hidden, weight):
    ny, nx = plan.ny, plan.nx
    pieces = []
    for d in range(plan.nz):
        piece = plan.send_z(out_grad, d) if d else out_grad
        if d == 1:
            weight, piece = plan.stage(weight, piece)
        elif d:
            piece = plan.relay(piece, [weight])
        pieces += [piece] + [plan.swap(piece, c) for c in range(1, CORES)]

    own, units = hidden.shape
    half = own // 2
    at_x = [hidden] + [plan.send_row(hidden, 0, dx) for dx in range(1, nx)]
    at_y = [hidden] + [plan.send_row(hidden, dy, 0) for dy in range(1, ny)]

    def block_of(dy, dx):
        if dy == 0:
            return [at_x[dx]]
        if dx == 0:
            return [at_y[dy]]
        return [plan.send_row(at_x[dx][:half], dy, 0), plan.send_row(at_y[dy][half:], 0, dx)]

    blocks = []
    for sy in range(ny):
        for sx in range(nx):
            blocks += block_of((ny - sy) % ny, (nx - sx) % nx)

    tile = 256 if units % 256 == 0 else 128
    chunks, rows = split(units, tile, 4), split(units, tile, 2)
    weight_grad = token_grad = None
    held = plan.gather_tokens(pieces, [])
    last, parts, lates, gathered = [], [], [], None

    def part(at):
        nonlocal last
        (first, width), x_first = chunks[at], at % 2 == 0
        messages, keep = plan.token_part(held, weight, first, width, 2 * tile, x_first, last)
        last = [keep]
        got = [plan.send_row(msg, 0, d + 1) if x_first else plan.send_row(msg, d + 1, 0) for d, msg in enumerate(messages)]
        parts.append((keep, got))

    def collect(at):
        nonlocal last, gathered
        gathered = plan.gather_hidden(blocks, last)
        last = [gathered]

    def join(at):
        nonlocal last
        x_first = at % 2 == 0
        keep, got = parts[at]
        onward = plan.combine(got, keep, ny if x_first else nx, last)
        last = list(onward[:1])
        lates.append([plan.send_row(msg, d + 1, 0) if x_first else plan.send_row(msg, 0, d + 1) for d, msg in enumerate(onward)])

    def weigh(at):
        nonlocal last, weight_grad
        first, width = rows[at]
        weight_grad, mark = plan.weight_part(held, gathered, first, width, tile, weight_grad, last)
        last = [mark]

    def end(at):
        nonlocal last, token_grad
        token_grad, mark = plan.finish(chunks[at][0], *parts[at], lates[at], own, units, token_grad, last)
        last = [mark]

    for name, at in PROGRAM:
        if at < len(chunks):
            {"part": part, "collect": collect, "join": join, "weigh": weigh, "end": end}[name](at)
    return token_grad, weight_grad


PROGRAM = [
    ("part", 0),
    ("part", 1),
    ("collect", 0),
    ("part", 2),
    ("part", 3),
    ("weigh", 0),
    ("join", 0),
    ("join", 1),
    ("join", 2),
    ("join", 3),
    ("weigh", 1),
    ("end", 0),
    ("end", 1),
    ("end", 2),
    ("end", 3),
]


def solution(mesh):
    return jax.shard_map(
        functools.partial(on_device, Plan(mesh)),
        mesh=mesh,
        in_specs=(P("col", "row"), P("row", "col"), P("col", "row")),
        out_specs=(P("row", "col"), P("col", "row")),
        check_vma=False,
    )
```

```python
import functools

import jax
import jax.numpy as jnp
from jax import lax
from jax.experimental import pallas as pl
from jax.experimental.pallas import tpu as pltpu
from jax.sharding import PartitionSpec as P

CORES = 2
SPAN = 120.0
SCALE_ROWS = 16
LANES = 128
TILE = 512
FLOPS = 2 * 10**9
SLOTS = 4
COST = 0
SCOPED = 20 * 1024 * 1024
ANY, HBM, VMEM = pl.ANY, pltpu.HBM, pltpu.VMEM
MARK = ((8, 128), jnp.float32, VMEM)


def call(kernel, name, operands, results, scratch=(), aliases={}, flops=0):
    return pl.pallas_call(
        kernel,
        in_specs=[pl.BlockSpec(memory_space=memory) for _, memory in operands],
        out_specs=[pl.BlockSpec(memory_space=memory) for _, _, memory in results],
        out_shape=[
            jax.ShapeDtypeStruct(shape, dtype) if memory is ANY else memory(shape, dtype)
            for shape, dtype, memory in results
        ],
        scratch_shapes=list(scratch),
        input_output_aliases=aliases,
        compiler_params=pltpu.CompilerParams(vmem_limit_bytes=SCOPED),
        cost_estimate=pl.CostEstimate(flops=flops, bytes_accessed=COST, transcendentals=0),
        name=name,
    )(*[pltpu.with_memory_space_constraint(array, memory) for array, memory in operands])


def grid_of(n):
    ny = int(n**0.5)
    while n % ny:
        ny -= 1
    return ny, n // ny


def message_shape(rows, width):
    runs = width // LANES
    return (runs * rows + -(-runs // SCALE_ROWS) * SCALE_ROWS, LANES)


def encode(blocks):
    top = functools.reduce(jnp.maximum, [jnp.max(jnp.abs(block), axis=0, keepdims=True) for block in blocks])
    scale = jnp.maximum(top * 1.0078125, 1e-36).astype(jnp.bfloat16).astype(jnp.float32)
    step = 2 * SPAN / scale
    codes = []
    for block in blocks:
        size = jnp.exp2(jnp.abs(block) * step - SPAN)
        codes.append(jnp.where(block < 0, -size, size).astype(jnp.bfloat16))
    return codes, scale


def store_codes(ref, first, blocks):
    codes, scale = encode(blocks)
    rows = sum(code.shape[0] for code in codes)
    scales = []
    for at in range(0, scale.shape[1], LANES):
        start = (first + at) // LANES * rows
        for code in codes:
            ref[start : start + code.shape[0], :] = code[:, at : at + LANES]
            start += code.shape[0]
        scales.append(scale[:, at : at + LANES])
    return scales


def store_scales(ref, scales):
    extra = -len(scales) % SCALE_ROWS
    full = jnp.concatenate(scales + [jnp.ones((extra, LANES), jnp.float32)] * (extra > 0), axis=0)
    ref[ref.shape[0] - full.shape[0] :, :] = full.astype(jnp.bfloat16)


def decode(ref, group, start, stop, width):
    runs = width // LANES
    scales = ref[runs * group :, :].astype(jnp.float32) * (0.5 / SPAN)
    values = []
    for run in range(runs):
        code = ref[run * group + start : run * group + stop, :].astype(jnp.float32)
        size = (jnp.log2(jnp.abs(code)) + SPAN) * scales[run : run + 1]
        values.append(jnp.where(code < 0, -size, size))
    return values


class Plan:
    def __init__(self, mesh):
        self.n, self.m = mesh.shape["row"], mesh.shape["col"]
        self.ny, self.nx = grid_of(self.n)
        self.nz = self.m // CORES
        self.turned = self.ny == self.nx
        self.n1, self.n2 = self.nx, self.ny

    def place(self):
        row, col = lax.axis_index("row"), lax.axis_index("col")
        return row // self.nx, row % self.nx, col // CORES, col % CORES

    def send_row(self, array, first, second):
        pairs = []
        for y in range(self.ny):
            for x in range(self.nx):
                for col in range(self.m):
                    dy, dx = (first, second) if self.turned and col % CORES % 2 else (second, first)
                    to = (y + dy) % self.ny * self.nx + (x + dx) % self.nx
                    pairs.append(((y * self.nx + x) * self.m + col, to * self.m + col))
        return lax.ppermute(array, ("row", "col"), pairs)

    def peer_z(self, z, d):
        return z ^ d if self.nz & (self.nz - 1) == 0 else (z + d) % self.nz

    def from_z(self, z, d):
        return z ^ d if self.nz & (self.nz - 1) == 0 else (z + self.nz - d) % self.nz

    def direct(self, d):
        return self.nz & (self.nz - 1) != 0 or d & (d - 1) == 0

    def send_z(self, array, d):
        pairs = [(z * CORES + c, self.peer_z(z, d) * CORES + c) for z in range(self.nz) for c in range(CORES)]
        return lax.ppermute(array, "col", pairs)

    def swap(self, array, d):
        pairs = [(z * CORES + c, z * CORES + (c + d) % CORES) for z in range(self.nz) for c in range(CORES)]
        return lax.ppermute(array, "col", pairs)

    def token_copies(self, pieces, held, sems):
        y, x, z, core = self.place()
        rows = pieces[0].shape[0]
        per = self.m // self.n
        copies = []
        for at in range(len(pieces)):
            d, c = at // CORES, at % CORES
            origin = self.from_z(z, d) * CORES + lax.rem(core + CORES - c, CORES)
            owner = origin // per
            dy = lax.rem(owner // self.nx + self.ny - y, self.ny)
            dx = lax.rem(owner % self.nx + self.nx - x, self.nx)
            turn = lax.rem(core, 2) if self.turned else 0
            slot = (dx + turn * (dy - dx)) * self.n2 + dy + turn * (dx - dy)
            start = pl.multiple_of((slot * per + origin % per) * rows, rows)
            copies.append(pltpu.make_async_copy(pieces[at], held.at[pl.ds(start, rows), :], sems.at[at]))
        return copies

    def hold(self, hidden, relay):
        def kernel(hidden_ref, *refs):
            out, _, sem = refs[-3:]
            copy = pltpu.make_async_copy(hidden_ref, out, sem)
            copy.start()
            copy.wait()

        return call(
            kernel,
            "hold",
            [(hidden, HBM), (relay, ANY)],
            [(hidden.shape, hidden.dtype, VMEM), (relay.shape, relay.dtype, ANY)],
            [pltpu.SemaphoreType.DMA],
            aliases={1: 1},
        )

    def stage(self, weight, relay):
        def kernel(weight_ref, *refs):
            out, _, sem = refs[-3:]
            copy = pltpu.make_async_copy(weight_ref, out, sem)
            copy.start()
            copy.wait()

        return call(
            kernel,
            "stage",
            [(weight, HBM), (relay, ANY)],
            [(weight.shape, weight.dtype, VMEM), (relay.shape, relay.dtype, ANY)],
            [pltpu.SemaphoreType.DMA],
            aliases={1: 1},
        )

    def relay(self, arrays, after):
        operands = [(array, ANY) for array in (*arrays, *after)]
        results = [(array.shape, array.dtype, ANY) for array in arrays]
        return list(call(lambda *refs: None, "relay", operands, results, aliases={at: at for at in range(len(arrays))}))

    def gather_tokens(self, pieces, after):
        count, (rows, depth) = len(pieces), pieces[0].shape

        def kernel(*refs):
            out, sems = refs[-2:]
            copies = self.token_copies(refs[:count], out, sems)
            for copy in copies:
                copy.start()
            for copy in copies:
                copy.wait()

        return call(
            kernel,
            "gather_tokens",
            [(piece, ANY) for piece in pieces] + [(array, ANY) for array in after],
            [((count * rows, depth), jnp.bfloat16, VMEM)],
            [pltpu.SemaphoreType.DMA((count,))],
        )[0]

    def token_part(self, held, weight, first, width, after, flops):
        tokens, depth = held.shape
        group = tokens // self.n1
        results = [(message_shape(group, width), jnp.bfloat16, VMEM)] * (self.n1 - 1) + [((group, width), jnp.float32, VMEM)]

        def kernel(held_ref, weight_ref, *refs):
            outs = refs[len(after) :]
            messages, keep = outs[:-1], outs[-1]
            scales = [[] for _ in messages]
            for at in range(0, width, TILE):
                size = min(TILE, width - at)
                total = lax.dot_general(
                    held_ref[...],
                    weight_ref[first + at : first + at + size, :],
                    (((1,), (1,)), ((), ())),
                    preferred_element_type=jnp.float32,
                )
                keep[:, at : at + size] = total[:group]
                for peer in range(1, self.n1):
                    scales[peer - 1] += store_codes(messages[peer - 1], at, [total[peer * group : (peer + 1) * group]])
            for message, rows in zip(messages, scales):
                store_scales(message, rows)

        operands = [(array, VMEM) for array in (held, weight, *after)]
        *messages, keep = call(kernel, "token_part", operands, results, flops=flops)
        return messages, keep

    def combine(self, got, keep, after):
        group, width = keep.shape
        own = group // self.n2
        operands = [(array, VMEM) for array in (*got, keep, *after)]

        def kernel(*refs):
            messages, keep_ref, outs = refs[: len(got)], refs[len(got)], refs[len(operands) :]
            for block in range(1, self.n2):
                start, stop = block * own, (block + 1) * own
                brought = [decode(message, group, start, stop, width) for message in messages]
                scales = []
                for run in range(width // LANES):
                    at = run * LANES
                    total = keep_ref[start:stop, at : at + LANES]
                    for values in brought:
                        total = total + values[run]
                    scales += store_codes(outs[block - 1], at, [total])
                store_scales(outs[block - 1], scales)

        return list(call(kernel, "combine", operands, [(message_shape(own, width), jnp.bfloat16, VMEM)] * (self.n2 - 1)))

    def finish(self, parts, lates, own, units, so_far, after):
        operands, scratch = [], []
        for (_, got, keep), late in zip(parts, lates):
            scratch.append(pltpu.VMEM((own, keep.shape[1]), jnp.bfloat16))
            operands += [(array, VMEM) for array in (keep, *got, *late)]
        extra = [(so_far, HBM)] if so_far is not None else []

        def kernel(*refs):
            out, _, *bufs, sems = refs[len(operands) + len(after) + len(extra) :]
            copies = []
            for index, ((first, got, keep), late) in enumerate(zip(parts, lates)):
                width = keep.shape[1]
                keep_ref, firsts = refs[0], refs[1 : 1 + len(got)]
                seconds = refs[1 + len(got) : 1 + len(got) + len(late)]
                refs = refs[1 + len(got) + len(late) :]
                brought = [decode(message, keep.shape[0], 0, own, width) for message in firsts]
                brought += [decode(message, own, 0, own, width) for message in seconds]
                for run in range(width // LANES):
                    columns = slice(run * LANES, (run + 1) * LANES)
                    total = keep_ref[:own, columns]
                    for values in brought:
                        total = total + values[run]
                    bufs[index][:, columns] = total.astype(jnp.bfloat16)
                copies.append(pltpu.make_async_copy(bufs[index], out.at[:, pl.ds(first, width)], sems.at[index]))
                copies[-1].start()
            for copy in copies:
                copy.wait()

        return call(
            kernel,
            "finish",
            operands + [(array, VMEM) for array in after] + extra,
            [((own, units), jnp.bfloat16, HBM), MARK],
            scratch + [pltpu.SemaphoreType.DMA((len(parts),))],
            aliases={len(operands) + len(after): 0} if extra else {},
        )

    def weight_part(self, held, blocks, first, width, tile, so_far, after):
        depth, units = held.shape[1], blocks[0].shape[1]
        steps = width // tile
        extra = [(so_far, HBM)] if so_far is not None else []
        operands = [(array, VMEM) for array in (held, *blocks, *after)]

        def kernel(held_ref, *refs):
            out, _, buf, sems = refs[-4:]
            pending = []
            for s in range(steps):
                if s >= SLOTS:
                    pending[s - SLOTS].wait()
                start = first + s * tile
                buf[s % SLOTS] = lax.dot_general(
                    jnp.concatenate([ref[:, start : start + tile] for ref in refs[: len(blocks)]], axis=0),
                    held_ref[...],
                    (((0,), (0,)), ((), ())),
                    preferred_element_type=jnp.float32,
                ).astype(jnp.bfloat16)
                pending.append(pltpu.make_async_copy(buf.at[s % SLOTS], out.at[pl.ds(start, tile), :], sems.at[s % SLOTS]))
                pending[-1].start()
            for copy in pending[-SLOTS:]:
                copy.wait()

        return call(
            kernel,
            "weight_part",
            operands + extra,
            [((units, depth), jnp.bfloat16, HBM), MARK],
            [pltpu.VMEM((SLOTS, tile, depth), jnp.bfloat16), pltpu.SemaphoreType.DMA((SLOTS,))],
            aliases={len(operands): 0} if extra else {},
        )


def cut(tiles, shares):
    ends = [round(tiles * sum(shares[: at + 1]) / sum(shares)) for at in range(len(shares))]
    return [(start, end) for start, end in zip([0, *ends], ends) if end > start]


def on_device(plan, out_grad, hidden, weight):
    n1, n2 = plan.n1, plan.n2
    own, units = hidden.shape
    near = [plan.send_row(hidden, s, 0) for s in range(1, n1)]
    far = {d: plan.send_z(out_grad, d) for d in range(1, plan.nz) if plan.direct(d)}
    swapped = [plan.swap(out_grad, c) for c in range(1, CORES)]
    hidden, swapped[0] = plan.hold(hidden, swapped[0])
    side = [plan.send_row(hidden, 0, s) for s in range(1, n2)]
    weight, swapped[0] = plan.stage(weight, swapped[0])
    far[1] = plan.relay([far[1]], [weight])[0]
    near = plan.relay(near, [far[1]])
    later = [d for d in far if d > 1]
    far.update(zip(later, plan.relay([far[d] for d in later], near)))
    pieces = [out_grad] + swapped
    for d in range(1, plan.nz):
        if d not in far:
            far[d] = plan.send_z(far[d & (d - 1)], d & -d)
        pieces += [far[d]] + [plan.swap(far[d], c) for c in range(1, CORES)]

    passed = [[plan.send_row(piece, 0, s) for s in range(1, n2)] for piece in near]
    came = [[hidden] + side] + [[piece] + on for piece, on in zip(near, passed)]
    blocks = [came[-e1 % n1][-e2 % n2] for e1 in range(n1) for e2 in range(n2)]

    tile = 256 if units % 256 == 0 else 128
    rounds = [(start * tile, (end - start) * tile) for start, end in cut(units // tile, ROUNDS)]
    runs = [(start * tile, (end - start) * tile) for start, end in cut(units // tile, RUNS)]

    weight_grad = token_grad = None
    held = plan.gather_tokens(pieces, [])
    last, parts, lates = [], [], []

    def part(at):
        nonlocal last
        messages, keep = plan.token_part(held, weight, *rounds[at], last, FLOPS if at <= WAIT else 0)
        last = [keep]
        if at == min(WAIT, len(rounds) - 1):
            messages = plan.relay(messages, sum(passed, []) + side)
        parts.append((rounds[at][0], [plan.send_row(m, s + 1, 0) for s, m in enumerate(messages)], keep))

    def join(at):
        nonlocal last
        onward = plan.combine(parts[at][1], parts[at][2], last)
        last = onward[:1]
        lates.append([plan.send_row(m, 0, s + 1) for s, m in enumerate(onward)])

    def weigh(at):
        nonlocal last, weight_grad
        weight_grad, mark = plan.weight_part(held, blocks, *runs[at], tile, weight_grad, last)
        last = [mark]

    def end(start, stop):
        nonlocal last, token_grad
        token_grad, mark = plan.finish(parts[start:stop], lates[start:stop], own, units, token_grad, last)
        last = [mark]

    for name, at in PROGRAM:
        if name == "part" and at < len(rounds):
            part(at)
        elif name == "join" and at < len(rounds):
            join(at)
        elif name == "weigh" and at < len(runs):
            weigh(at)
        elif name == "end" and at < len(rounds):
            end(at, min(at + ENDS, len(rounds)))
    return token_grad, weight_grad


ROUNDS = (4, 4, 4, 2)
RUNS = (7, 4, 3)
ENDS = 2
WAIT = 1
PROGRAM = [
    ("part", 0),
    ("part", 1),
    ("part", 2),
    ("part", 3),
    ("weigh", 0),
    ("join", 0),
    ("join", 1),
    ("weigh", 1),
    ("join", 2),
    ("join", 3),
    ("end", 0),
    ("weigh", 2),
    ("end", 2),
]


def solution(mesh):
    return jax.shard_map(
        functools.partial(on_device, Plan(mesh)),
        mesh=mesh,
        in_specs=(P("col", "row"), P("row", "col"), P("col", "row")),
        out_specs=(P("row", "col"), P("col", "row")),
        check_vma=False,
    )
```

```python
import functools

import jax
import jax.numpy as jnp
from jax import lax
from jax.experimental import pallas as pl
from jax.experimental.pallas import tpu as pltpu
from jax.sharding import PartitionSpec as P

CORES = 2
SPAN = 120.0
SCALE_ROWS = 16
LANES = 128
TILE = 512
FLOPS = 2 * 10**9
SLOTS = 4
COST = 0
SCOPED = 20 * 1024 * 1024
ANY, HBM, VMEM = pl.ANY, pltpu.HBM, pltpu.VMEM
MARK = ((8, 128), jnp.float32, VMEM)


def call(kernel, name, operands, results, scratch=(), aliases={}, flops=0):
    return pl.pallas_call(
        kernel,
        in_specs=[pl.BlockSpec(memory_space=memory) for _, memory in operands],
        out_specs=[pl.BlockSpec(memory_space=memory) for _, _, memory in results],
        out_shape=[
            jax.ShapeDtypeStruct(shape, dtype) if memory is ANY else memory(shape, dtype)
            for shape, dtype, memory in results
        ],
        scratch_shapes=list(scratch),
        input_output_aliases=aliases,
        compiler_params=pltpu.CompilerParams(vmem_limit_bytes=SCOPED),
        cost_estimate=pl.CostEstimate(flops=flops, bytes_accessed=COST, transcendentals=0),
        name=name,
    )(*[pltpu.with_memory_space_constraint(array, memory) for array, memory in operands])


def grid_of(n):
    ny = int(n**0.5)
    while n % ny:
        ny -= 1
    return ny, n // ny


def message_shape(rows, width):
    runs = width // LANES
    return (runs * rows + -(-runs // SCALE_ROWS) * SCALE_ROWS, LANES)


def encode(blocks):
    top = functools.reduce(jnp.maximum, [jnp.max(jnp.abs(block), axis=0, keepdims=True) for block in blocks])
    scale = jnp.maximum(top * 1.0078125, 1e-36).astype(jnp.bfloat16).astype(jnp.float32)
    step = 2 * SPAN / scale
    codes = []
    for block in blocks:
        size = jnp.exp2(jnp.abs(block) * step - SPAN)
        codes.append(jnp.where(block < 0, -size, size).astype(jnp.bfloat16))
    return codes, scale


def store_codes(ref, first, blocks):
    codes, scale = encode(blocks)
    rows = sum(code.shape[0] for code in codes)
    scales = []
    for at in range(0, scale.shape[1], LANES):
        start = (first + at) // LANES * rows
        for code in codes:
            ref[start : start + code.shape[0], :] = code[:, at : at + LANES]
            start += code.shape[0]
        scales.append(scale[:, at : at + LANES])
    return scales


def store_scales(ref, scales):
    extra = -len(scales) % SCALE_ROWS
    full = jnp.concatenate(scales + [jnp.ones((extra, LANES), jnp.float32)] * (extra > 0), axis=0)
    ref[ref.shape[0] - full.shape[0] :, :] = full.astype(jnp.bfloat16)


def decode(ref, group, start, stop, width):
    runs = width // LANES
    scales = ref[runs * group :, :].astype(jnp.float32) * (0.5 / SPAN)
    values = []
    for run in range(runs):
        code = ref[run * group + start : run * group + stop, :].astype(jnp.float32)
        size = (jnp.log2(jnp.abs(code)) + SPAN) * scales[run : run + 1]
        values.append(jnp.where(code < 0, -size, size))
    return values


class Plan:
    def __init__(self, mesh):
        self.n, self.m = mesh.shape["row"], mesh.shape["col"]
        self.ny, self.nx = grid_of(self.n)
        self.nz = self.m // CORES
        self.turned = self.ny == self.nx
        self.n1, self.n2 = self.nx, self.ny

    def place(self):
        row, col = lax.axis_index("row"), lax.axis_index("col")
        return row // self.nx, row % self.nx, col // CORES, col % CORES

    def send_row(self, array, first, second):
        pairs = []
        for y in range(self.ny):
            for x in range(self.nx):
                for col in range(self.m):
                    dy, dx = (first, second) if self.turned and col % CORES % 2 else (second, first)
                    to = (y + dy) % self.ny * self.nx + (x + dx) % self.nx
                    pairs.append(((y * self.nx + x) * self.m + col, to * self.m + col))
        return lax.ppermute(array, ("row", "col"), pairs)

    def peer_z(self, z, d):
        return z ^ d if self.nz & (self.nz - 1) == 0 else (z + d) % self.nz

    def from_z(self, z, d):
        return z ^ d if self.nz & (self.nz - 1) == 0 else (z + self.nz - d) % self.nz

    def direct(self, d):
        return self.nz & (self.nz - 1) != 0 or d & (d - 1) == 0

    def send_z(self, array, d):
        pairs = [(z * CORES + c, self.peer_z(z, d) * CORES + c) for z in range(self.nz) for c in range(CORES)]
        return lax.ppermute(array, "col", pairs)

    def swap(self, array, d):
        pairs = [(z * CORES + c, z * CORES + (c + d) % CORES) for z in range(self.nz) for c in range(CORES)]
        return lax.ppermute(array, "col", pairs)

    def token_copies(self, pieces, held, sems):
        y, x, z, core = self.place()
        rows = pieces[0].shape[0]
        per = self.m // self.n
        copies = []
        for at in range(len(pieces)):
            d, c = at // CORES, at % CORES
            origin = self.from_z(z, d) * CORES + lax.rem(core + CORES - c, CORES)
            owner = origin // per
            dy = lax.rem(owner // self.nx + self.ny - y, self.ny)
            dx = lax.rem(owner % self.nx + self.nx - x, self.nx)
            turn = lax.rem(core, 2) if self.turned else 0
            slot = (dx + turn * (dy - dx)) * self.n2 + dy + turn * (dx - dy)
            start = pl.multiple_of((slot * per + origin % per) * rows, rows)
            copies.append(pltpu.make_async_copy(pieces[at], held.at[pl.ds(start, rows), :], sems.at[at]))
        return copies

    def hold(self, hidden, relay):
        def kernel(hidden_ref, *refs):
            out, _, sem = refs[-3:]
            copy = pltpu.make_async_copy(hidden_ref, out, sem)
            copy.start()
            copy.wait()

        return call(
            kernel,
            "hold",
            [(hidden, HBM), (relay, ANY)],
            [(hidden.shape, hidden.dtype, VMEM), (relay.shape, relay.dtype, ANY)],
            [pltpu.SemaphoreType.DMA],
            aliases={1: 1},
        )

    def stage(self, weight, relay):
        def kernel(weight_ref, *refs):
            out, _, sem = refs[-3:]
            copy = pltpu.make_async_copy(weight_ref, out, sem)
            copy.start()
            copy.wait()

        return call(
            kernel,
            "stage",
            [(weight, HBM), (relay, ANY)],
            [(weight.shape, weight.dtype, VMEM), (relay.shape, relay.dtype, ANY)],
            [pltpu.SemaphoreType.DMA],
            aliases={1: 1},
        )

    def relay(self, arrays, after):
        operands = [(array, ANY) for array in (*arrays, *after)]
        results = [(array.shape, array.dtype, ANY) for array in arrays]
        return list(call(lambda *refs: None, "relay", operands, results, aliases={at: at for at in range(len(arrays))}))

    def gather_tokens(self, pieces, after):
        count, (rows, depth) = len(pieces), pieces[0].shape

        def kernel(*refs):
            out, sems = refs[-2:]
            copies = self.token_copies(refs[:count], out, sems)
            for copy in copies:
                copy.start()
            for copy in copies:
                copy.wait()

        return call(
            kernel,
            "gather_tokens",
            [(piece, ANY) for piece in pieces] + [(array, ANY) for array in after],
            [((count * rows, depth), jnp.bfloat16, VMEM)],
            [pltpu.SemaphoreType.DMA((count,))],
        )[0]

    def token_part(self, held, weight, first, width, after, flops):
        tokens, depth = held.shape
        group = tokens // self.n1
        results = [(message_shape(group, width), jnp.bfloat16, VMEM)] * (self.n1 - 1) + [((group, width), jnp.float32, VMEM)]

        def kernel(held_ref, weight_ref, *refs):
            outs = refs[len(after) :]
            messages, keep = outs[:-1], outs[-1]
            scales = [[] for _ in messages]
            for at in range(0, width, TILE):
                size = min(TILE, width - at)
                total = lax.dot_general(
                    held_ref[...],
                    weight_ref[first + at : first + at + size, :],
                    (((1,), (1,)), ((), ())),
                    preferred_element_type=jnp.float32,
                )
                keep[:, at : at + size] = total[:group]
                for peer in range(1, self.n1):
                    scales[peer - 1] += store_codes(messages[peer - 1], at, [total[peer * group : (peer + 1) * group]])
            for message, rows in zip(messages, scales):
                store_scales(message, rows)

        operands = [(array, VMEM) for array in (held, weight, *after)]
        *messages, keep = call(kernel, "token_part", operands, results, flops=flops)
        return messages, keep

    def combine(self, got, keep, after):
        group, width = keep.shape
        own = group // self.n2
        operands = [(array, VMEM) for array in (*got, keep, *after)]

        def kernel(*refs):
            messages, keep_ref, outs = refs[: len(got)], refs[len(got)], refs[len(operands) :]
            for block in range(1, self.n2):
                start, stop = block * own, (block + 1) * own
                brought = [decode(message, group, start, stop, width) for message in messages]
                scales = []
                for run in range(width // LANES):
                    at = run * LANES
                    total = keep_ref[start:stop, at : at + LANES]
                    for values in brought:
                        total = total + values[run]
                    scales += store_codes(outs[block - 1], at, [total])
                store_scales(outs[block - 1], scales)

        return list(call(kernel, "combine", operands, [(message_shape(own, width), jnp.bfloat16, VMEM)] * (self.n2 - 1)))

    def finish(self, parts, lates, own, units, so_far, after):
        operands, scratch = [], []
        for (_, got, keep), late in zip(parts, lates):
            scratch.append(pltpu.VMEM((own, keep.shape[1]), jnp.bfloat16))
            operands += [(array, VMEM) for array in (keep, *got, *late)]
        extra = [(so_far, HBM)] if so_far is not None else []

        def kernel(*refs):
            out, _, *bufs, sems = refs[len(operands) + len(after) + len(extra) :]
            copies = []
            for index, ((first, got, keep), late) in enumerate(zip(parts, lates)):
                width = keep.shape[1]
                keep_ref, firsts = refs[0], refs[1 : 1 + len(got)]
                seconds = refs[1 + len(got) : 1 + len(got) + len(late)]
                refs = refs[1 + len(got) + len(late) :]
                brought = [decode(message, keep.shape[0], 0, own, width) for message in firsts]
                brought += [decode(message, own, 0, own, width) for message in seconds]
                for run in range(width // LANES):
                    columns = slice(run * LANES, (run + 1) * LANES)
                    total = keep_ref[:own, columns]
                    for values in brought:
                        total = total + values[run]
                    bufs[index][:, columns] = total.astype(jnp.bfloat16)
                copies.append(pltpu.make_async_copy(bufs[index], out.at[:, pl.ds(first, width)], sems.at[index]))
                copies[-1].start()
            for copy in copies:
                copy.wait()

        return call(
            kernel,
            "finish",
            operands + [(array, VMEM) for array in after] + extra,
            [((own, units), jnp.bfloat16, HBM), MARK],
            scratch + [pltpu.SemaphoreType.DMA((len(parts),))],
            aliases={len(operands) + len(after): 0} if extra else {},
        )

    def weight_part(self, held, blocks, first, width, tile, so_far, after):
        depth, units = held.shape[1], blocks[0].shape[1]
        steps = width // tile
        extra = [(so_far, HBM)] if so_far is not None else []
        operands = [(array, VMEM) for array in (held, *blocks, *after)]

        def kernel(held_ref, *refs):
            out, _, buf, sems = refs[-4:]
            pending = []
            for s in range(steps):
                if s >= SLOTS:
                    pending[s - SLOTS].wait()
                start = first + s * tile
                buf[s % SLOTS] = lax.dot_general(
                    jnp.concatenate([ref[:, start : start + tile] for ref in refs[: len(blocks)]], axis=0),
                    held_ref[...],
                    (((0,), (0,)), ((), ())),
                    preferred_element_type=jnp.float32,
                ).astype(jnp.bfloat16)
                pending.append(pltpu.make_async_copy(buf.at[s % SLOTS], out.at[pl.ds(start, tile), :], sems.at[s % SLOTS]))
                pending[-1].start()
            for copy in pending[-SLOTS:]:
                copy.wait()

        return call(
            kernel,
            "weight_part",
            operands + extra,
            [((units, depth), jnp.bfloat16, HBM), MARK],
            [pltpu.VMEM((SLOTS, tile, depth), jnp.bfloat16), pltpu.SemaphoreType.DMA((SLOTS,))],
            aliases={len(operands): 0} if extra else {},
        )


def cut(tiles, shares):
    ends = [round(tiles * sum(shares[: at + 1]) / sum(shares)) for at in range(len(shares))]
    return [(start, end) for start, end in zip([0, *ends], ends) if end > start]


def on_device(plan, out_grad, hidden, weight):
    n1, n2 = plan.n1, plan.n2
    own, units = hidden.shape
    near = [plan.send_row(hidden, s, 0) for s in range(1, n1)]
    far = {d: plan.send_z(out_grad, d) for d in range(1, plan.nz) if plan.direct(d)}
    swapped = [plan.swap(out_grad, c) for c in range(1, CORES)]
    hidden, swapped[0] = plan.hold(hidden, swapped[0])
    side = [plan.send_row(hidden, 0, s) for s in range(1, n2)]
    weight, swapped[0] = plan.stage(weight, swapped[0])
    far[1] = plan.relay([far[1]], [weight])[0]
    later = [d for d in far if d > 1]
    far.update(zip(later, plan.relay([far[d] for d in later], [far[1]])))
    near = plan.relay(near, [far[1]])
    pieces = [out_grad] + swapped
    for d in range(1, plan.nz):
        if d not in far:
            far[d] = plan.send_z(far[d & (d - 1)], d & -d)
        pieces += [far[d]] + [plan.swap(far[d], c) for c in range(1, CORES)]

    passed = [[plan.send_row(piece, 0, s) for s in range(1, n2)] for piece in near]
    came = [[hidden] + side] + [[piece] + on for piece, on in zip(near, passed)]
    blocks = [came[-e1 % n1][-e2 % n2] for e1 in range(n1) for e2 in range(n2)]

    tile = 256 if units % 256 == 0 else 128
    rounds = [(start * tile, (end - start) * tile) for start, end in cut(units // tile, ROUNDS)]
    runs = [(start * tile, (end - start) * tile) for start, end in cut(units // tile, RUNS)]

    weight_grad = token_grad = None
    held = plan.gather_tokens(pieces, [])
    last, parts, lates = [], [], []

    def part(at):
        nonlocal last
        messages, keep = plan.token_part(held, weight, *rounds[at], last, FLOPS if at <= WAIT else 0)
        last = [keep]
        if at == min(WAIT, len(rounds) - 1):
            messages = plan.relay(messages, sum(passed, []) + side)
        parts.append((rounds[at][0], [plan.send_row(m, s + 1, 0) for s, m in enumerate(messages)], keep))

    def join(at):
        nonlocal last
        onward = plan.combine(parts[at][1], parts[at][2], last)
        last = onward[:1]
        lates.append([plan.send_row(m, 0, s + 1) for s, m in enumerate(onward)])

    def weigh(at):
        nonlocal last, weight_grad
        weight_grad, mark = plan.weight_part(held, blocks, *runs[at], tile, weight_grad, last)
        last = [mark]

    def end(start, stop):
        nonlocal last, token_grad
        token_grad, mark = plan.finish(parts[start:stop], lates[start:stop], own, units, token_grad, last)
        last = [mark]

    for name, at in PROGRAM:
        if name == "part" and at < len(rounds):
            part(at)
        elif name == "join" and at < len(rounds):
            join(at)
        elif name == "weigh" and at < len(runs):
            weigh(at)
        elif name == "end" and at < len(rounds):
            end(at, min(at + ENDS, len(rounds)))
    return token_grad, weight_grad


ROUNDS = (4, 4, 4, 2)
RUNS = (7, 6, 1)
ENDS = 2
WAIT = 1
PROGRAM = [
    ("part", 0),
    ("part", 1),
    ("part", 2),
    ("part", 3),
    ("weigh", 0),
    ("join", 0),
    ("join", 1),
    ("weigh", 1),
    ("join", 2),
    ("join", 3),
    ("end", 0),
    ("weigh", 2),
    ("end", 2),
]


def solution(mesh):
    return jax.shard_map(
        functools.partial(on_device, Plan(mesh)),
        mesh=mesh,
        in_specs=(P("col", "row"), P("row", "col"), P("col", "row")),
        out_specs=(P("row", "col"), P("col", "row")),
        check_vma=False,
    )
```
